32 devices in a mesh: parts: 2 (over y), fsdp: 8 (over z, x), clients: 2 (over core).
Axes of the slice: x: 2, y: 2, z: 4, core: 2. Of those that a mesh axis runs over, the one named last changes fastest.
Arguments:
- pool_x: bfloat16 [32768, 2560], P(('parts', 'fsdp')), parts along dimension 0, may hold values from -6 to 6
- pool_cot: bfloat16 [32768, 1024], P(('parts', 'fsdp')), parts along dimension 0, may hold values from -0.06591797 to 0.06591797
- assignment: int32 [16, 2048], P(('parts', 'fsdp'), 'clients'), parts along dimension 0, may hold values from 0 to 2047, each once within a row
- weight: float32 [2560, 1024], P('fsdp'), may hold values from -0.125 to 0.125
- gain: float32 [128], replicated, may hold values from 0.1 to 1.9
- global_variate: float32 [5120, 1024], P(('parts', 'fsdp')), parts along dimension 0, may hold values from -6 to 6
- client_variate: float32 [4, 2560, 1024], P(('parts', 'clients'), 'fsdp'), parts along dimension 0, may hold values from -6 to 6
Outputs:
- new_weight: float32 [5120, 1024], P(('parts', 'fsdp')), parts along dimension 0
- new_global: float32 [5120, 1024], P(('parts', 'fsdp')), parts along dimension 0
- new_client: float32 [4, 2560, 1024], P(('parts', 'clients'), 'fsdp'), parts along dimension 0
The draws below stay inside these ranges and needn't reach their ends.
There are 2 independent parts, one for each index of `parts`. The reference program is written for one: setup_inputs(seed, part) draws one part's arguments, and reference() takes and returns one part's arrays. A program takes and returns all parts, laid end to end along the dimension named above; an argument that names none is the same for every part. Nothing has to cross between parts.
Inputs may be any that keep to these rules, and one draw needn't show every extreme that they name: Each row of assignment holds every local pool row index once.
All inputs are finite; a program needn't handle non-finite values.
Results may differ from the reference program's by a relative error of at most 0.0029.
Values may be sent and summed in bfloat16 or wider, within the bound.
A program may use at most 128 MiB of HBM per device.

```python
import jax
import jax.numpy as jnp
from jax import lax

D = 2560
KV_HEADS = 8
HEAD = 128
TOK_DEV = 1024
KW = 1024
POOL = 16384
N_FSDP = 8
N_CLIENTS = 2


def with_spikes(drawn, rng, source, target, parts, factor):
    owner, partner = [(jnp.arange(drawn.shape[dim]) // (drawn.shape[dim] // parts)).reshape([-1 if axis == dim else 1 for axis in range(drawn.ndim)]) for dim in (source, target)]
    chosen = jax.random.permutation(rng, parts)[partner]
    strong = (owner == chosen) | (owner == (partner + parts // 2) % parts)
    return jnp.where(strong, factor * drawn, drawn)


def levels(key, dims, pieces, low, high):
    factor_of = 1.0
    for axis_at, shards_of in pieces:
        steps = jax.random.uniform(jax.random.fold_in(jax.random.fold_in(key, 6), axis_at), (shards_of,), jnp.float32, low / len(pieces), high / len(pieces))
        factor_of = factor_of * jnp.repeat(jnp.exp(steps), dims[axis_at] // shards_of).reshape((-1,) + (1,) * (len(dims) - 1 - axis_at))
    return factor_of


def centred(rng, dims, deviation, reach, pieces=(), held_as=jnp.bfloat16):
    array = jax.random.normal(rng, dims, jnp.float32) * deviation
    if len(pieces) > 0:
        array = levels(rng, dims, pieces, -0.22, 0.18) * array
    return jnp.clip(array, min=-reach, max=reach).astype(held_as)


def noise_with(rng, extent, width, reach, cuts, heavy, kind=jnp.bfloat16):
    values = width * jax.random.normal(rng, extent, jnp.float32)
    if cuts:
        values = values * levels(rng, extent, cuts, -0.22, 0.18)
    return jnp.clip(with_spikes(values, jax.random.fold_in(rng, 3), *heavy), -reach, reach).astype(kind)


def setup_inputs(seed: int = 0, part: int = 0) -> dict:
    arg_keys = jax.random.split(jax.random.key(seed), 8)
    part_keys = jax.random.split(jax.random.fold_in(arg_keys[7], part), 8)
    pool_x = noise_with(part_keys[0], (POOL, D), 1.0, 6.0, ((0, 8),), (0, 1, 8, 2.0))
    pool_cot = centred(part_keys[1], (POOL, KW), (1.0 / (TOK_DEV * N_FSDP) ** 0.5), 0.06591797, ((0, 8),))
    assignment = jax.vmap(lambda own: jax.random.permutation(own, N_CLIENTS * TOK_DEV))(jax.random.split(part_keys[2], N_FSDP)).reshape((N_FSDP, N_CLIENTS * TOK_DEV)).astype(jnp.int32)
    weight = centred(arg_keys[3], (D, KW), D ** -0.5, 0.125, ((0, 8),), jnp.float32)
    gain = jnp.clip(1.0 + 0.18 * jax.random.normal(arg_keys[4], (HEAD,), jnp.float32), 0.1, 1.9)
    global_variate = centred(part_keys[5], (D, KW), 1.0, 6.0, ((0, 8),), jnp.float32)
    client_variate = centred(part_keys[6], (N_CLIENTS, D, KW), 1.0, 6.0, ((0, 2), (1, 8)), jnp.float32)
    return {"pool_x": pool_x, "pool_cot": pool_cot, "assignment": assignment, "weight": weight, "gain": gain, "global_variate": global_variate, "client_variate": client_variate}


norm_eps = 1e-06
local_rate = 0.05

def norm_backward(keys, cotangent, gain):
    count = keys.shape[0]
    heads = keys.reshape(count, KV_HEADS, HEAD)
    inverse = lax.rsqrt(lax.optimization_barrier(jnp.mean(heads * heads, axis=-1, keepdims=True)) + norm_eps)
    scaled = cotangent.astype(jnp.float32).reshape(count, KV_HEADS, HEAD) * gain.astype(jnp.float32)
    along = lax.optimization_barrier(jnp.sum(scaled * heads, axis=-1, keepdims=True))
    result = scaled * inverse - heads * along * inverse * inverse * inverse / HEAD
    return result.reshape(count, KV_HEADS * HEAD).astype(jnp.bfloat16)

def reference(pool_x, pool_cot, assignment, weight, gain, global_variate, client_variate):
    per_device = N_CLIENTS * TOK_DEV
    offsets = (jnp.arange(N_FSDP, dtype=jnp.int32) * per_device)[:, None]
    all_rows = assignment.astype(jnp.int32) + offsets
    weight_b = weight.astype(jnp.bfloat16)

    def one_client(index):
        picked = lax.dynamic_slice_in_dim(all_rows, index * TOK_DEV, TOK_DEV, 1).reshape(-1)
        x_rows = jnp.take(pool_x, picked, axis=0)
        cot_rows = jnp.take(pool_cot, picked, axis=0)
        keys = jnp.dot(x_rows, weight_b, preferred_element_type=jnp.float32)
        dkeys = norm_backward(keys, cot_rows, gain)
        return jnp.dot(x_rows.T, dkeys, preferred_element_type=jnp.float32)
    grads = lax.map(one_client, jnp.arange(N_CLIENTS, dtype=jnp.int32))
    delta = -local_rate * (grads - client_variate + global_variate[None])
    change = grads - client_variate
    new_weight = weight + lax.optimization_barrier(jnp.sum(delta, axis=0)) / N_CLIENTS
    new_global = global_variate + lax.optimization_barrier(jnp.sum(change, axis=0)) / N_CLIENTS
    return (new_weight, new_global, grads)
```

```python
import jax
import jax.numpy as jnp
from jax import lax
from jax.sharding import PartitionSpec as P

HEAD = 128

norm_eps = 1e-06
local_rate = 0.05
CHUNKS = 4


def norm_backward(keys, cotangent, gain):
    count, width = keys.shape
    heads = keys.reshape(count, width // HEAD, HEAD)
    inverse = lax.rsqrt(jnp.mean(heads * heads, axis=-1, keepdims=True) + norm_eps)
    scaled = cotangent.astype(jnp.float32).reshape(heads.shape) * gain
    along = jnp.sum(scaled * heads, axis=-1, keepdims=True)
    result = scaled * inverse - heads * along * inverse * inverse * inverse / HEAD
    return result.reshape(count, width).astype(jnp.bfloat16)


def gather_weight(weight):
    weight_b = weight.astype(jnp.bfloat16)
    members = lax.axis_size("clients")
    parts = lax.axis_size("parts")
    rows = weight.shape[0] // (members * parts)
    place = lax.axis_index("clients") * parts + lax.axis_index("parts")
    own = lax.dynamic_slice_in_dim(weight_b, place * rows, rows, 0)
    return lax.all_gather(own, ("fsdp", "clients", "parts"), axis=0, tiled=True)


def scatter_sum(partial):
    n = lax.axis_size("fsdp")
    lines = n // 2
    me = lax.axis_index("fsdp")
    line, side = me // 2, lax.rem(me, 2)
    rows = partial.shape[0] // n
    blocks = partial.reshape(lines, 2, rows, partial.shape[1])
    away = lax.dynamic_index_in_dim(blocks, 1 - side, 1, keepdims=False)
    home = lax.dynamic_index_in_dim(blocks, side, 1, keepdims=False)
    came = lax.ppermute(
        away.astype(jnp.bfloat16), "fsdp", [(i, i ^ 1) for i in range(n)]
    )
    both = home + came.astype(jnp.float32)
    own = lax.dynamic_index_in_dim(both, line, 0, keepdims=False)
    if lines <= 4:
        total = own
        for step in range(1, lines):
            block = lax.dynamic_index_in_dim(
                both, lax.rem(line + step, lines), 0, keepdims=False
            )
            pairs = [(i, (i + 2 * step) % n) for i in range(n)]
            got = lax.ppermute(block.astype(jnp.bfloat16), "fsdp", pairs)
            total = total + got.astype(jnp.float32)
        return total
    groups = [[2 * z + x for z in range(lines)] for x in range(2)]
    got = lax.all_to_all(
        both.astype(jnp.bfloat16), "fsdp", 0, 0, axis_index_groups=groups
    ).astype(jnp.float32)
    others = jnp.arange(lines)[:, None, None] != line
    return own + jnp.sum(jnp.where(others, got, 0.0), axis=0)


def per_device(pool_x, pool_cot, assignment, weight, gain, global_variate, client_variate):
    members = lax.axis_size("clients")
    weight_b = gather_weight(weight)
    picked = assignment[0]
    x_rows = jnp.take(pool_x, picked, axis=0)
    cot_rows = jnp.take(pool_cot, picked, axis=0)
    width = weight.shape[1] // CHUNKS
    own_variate = client_variate[0]
    results = []
    for chunk in range(CHUNKS):
        cut = slice(chunk * width, (chunk + 1) * width)
        keys = jnp.dot(x_rows, weight_b[:, cut], preferred_element_type=jnp.float32)
        dkeys = norm_backward(keys, cot_rows[:, cut], gain)
        partial = lax.dot_general(
            x_rows, dkeys, (((0,), (0,)), ((), ())), preferred_element_type=jnp.float32
        )
        grads = scatter_sum(partial)
        change = grads - own_variate[:, cut]
        total_change = change
        for step in range(1, members):
            pairs = [(i, (i + step) % members) for i in range(members)]
            total_change = total_change + lax.ppermute(change, "clients", pairs)
        common = global_variate[:, cut]
        total_delta = -local_rate * (total_change + members * common)
        new_weight = weight[:, cut] + total_delta / members
        new_global = common + total_change / members
        results.append((new_weight, new_global, grads))
    new_weight, new_global, grads = (
        jnp.concatenate(list(pieces), axis=1) for pieces in zip(*results)
    )
    return (new_weight, new_global, grads[None])


def solution(mesh):
    placed = (
        P(("parts", "fsdp"), None),
        P(("parts", "fsdp"), None),
        P(("parts", "fsdp"), "clients"),
        P("fsdp", None),
        P(),
        P(("parts", "fsdp"), None),
        P(("parts", "clients"), "fsdp", None),
    )
    return jax.shard_map(
        per_device,
        mesh=mesh,
        in_specs=placed,
        out_specs=(
            P(("parts", "fsdp"), None),
            P(("parts", "fsdp"), None),
            P(("parts", "clients"), "fsdp", None),
        ),
        check_vma=False,
    )
```

```python
import jax
import jax.numpy as jnp
from jax import lax
from jax.sharding import PartitionSpec as P

HEAD = 128

norm_eps = 1e-06
local_rate = 0.05
CHUNKS = 4


def norm_backward(keys, cotangent, gain):
    count, width = keys.shape
    heads = keys.reshape(count, width // HEAD, HEAD)
    inverse = lax.rsqrt(jnp.mean(heads * heads, axis=-1, keepdims=True) + norm_eps)
    scaled = cotangent.astype(jnp.float32).reshape(heads.shape) * gain
    along = jnp.sum(scaled * heads, axis=-1, keepdims=True)
    result = scaled * inverse - heads * along * inverse * inverse * inverse / HEAD
    return result.reshape(count, width).astype(jnp.bfloat16)


def gather_weight(weight):
    weight_b = weight.astype(jnp.bfloat16)
    rows = weight.shape[0] // lax.axis_size("clients")
    own = lax.dynamic_slice_in_dim(weight_b, lax.axis_index("clients") * rows, rows, 0)
    width = weight.shape[1] // CHUNKS
    chunks = []
    for chunk in range(CHUNKS):
        piece = own[:, chunk * width : (chunk + 1) * width]
        chunks.append(lax.all_gather(piece, ("fsdp", "clients"), axis=0, tiled=True))
    return chunks


def scatter_sum(partial, before):
    n = lax.axis_size("fsdp")
    lines = n // 2
    me = lax.axis_index("fsdp")
    line, side = me // 2, lax.rem(me, 2)
    rows = partial.shape[0] // n
    blocks = partial.reshape(lines, 2, rows, partial.shape[1])
    away = lax.dynamic_index_in_dim(blocks, 1 - side, 1, keepdims=False)
    home = lax.dynamic_index_in_dim(blocks, side, 1, keepdims=False)
    away = away.astype(jnp.bfloat16)
    ready = lax.optimization_barrier((away, *before))[0] if before else away
    came = lax.ppermute(ready, "fsdp", [(i, i ^ 1) for i in range(n)])
    both = home + came.astype(jnp.float32)
    own = lax.dynamic_index_in_dim(both, line, 0, keepdims=False)
    if lines <= 4:
        total, moved = own, []
        for step in range(1, lines):
            block = lax.dynamic_index_in_dim(
                both, lax.rem(line + step, lines), 0, keepdims=False
            )
            pairs = [(i, (i + 2 * step) % n) for i in range(n)]
            got = lax.ppermute(block.astype(jnp.bfloat16), "fsdp", pairs)
            moved.append(got)
            total = total + got.astype(jnp.float32)
        return total, came, away, moved
    groups = [[2 * z + x for z in range(lines)] for x in range(2)]
    got = lax.all_to_all(
        both.astype(jnp.bfloat16), "fsdp", 0, 0, axis_index_groups=groups
    ).astype(jnp.float32)
    others = jnp.arange(lines)[:, None, None] != line
    return own + jnp.sum(jnp.where(others, got, 0.0), axis=0), came, away, []


def per_device(pool_x, pool_cot, assignment, weight, gain, global_variate, client_variate):
    members = lax.axis_size("clients")
    weight_b = gather_weight(weight)
    picked = assignment[0]
    x_rows = pool_x.at[picked].get(mode="promise_in_bounds")
    cot_rows = pool_cot.at[picked].get(mode="promise_in_bounds")
    width = weight.shape[1] // CHUNKS
    own_variate = client_variate[0]
    results, came, moved = [], [], []
    for chunk in range(CHUNKS):
        cut = slice(chunk * width, (chunk + 1) * width)
        weight_c = weight_b[chunk]
        if chunk:
            weight_c = lax.optimization_barrier((weight_c, sent))[0]
        keys = jnp.dot(x_rows, weight_c, preferred_element_type=jnp.float32)
        dkeys = norm_backward(keys, cot_rows[:, cut], gain)
        partial = lax.dot_general(
            x_rows, dkeys, (((0,), (0,)), ((), ())), preferred_element_type=jnp.float32
        )
        before = [came[chunk - 1]] if chunk >= 1 else []
        if chunk >= 2:
            before += moved[chunk - 2]
        grads, arrived, sent, along = scatter_sum(partial, before)
        came.append(arrived)
        moved.append(along)
        change = grads - own_variate[:, cut]
        total_change = change
        for step in range(1, members):
            pairs = [(i, (i + step) % members) for i in range(members)]
            total_change = total_change + lax.ppermute(change, "clients", pairs)
        common = global_variate[:, cut]
        total_delta = -local_rate * (total_change + members * common)
        new_weight = weight[:, cut] + total_delta / members
        new_global = common + total_change / members
        results.append((new_weight, new_global, grads))
    new_weight, new_global, grads = (
        jnp.concatenate(list(pieces), axis=1) for pieces in zip(*results)
    )
    return (new_weight, new_global, grads[None])


def solution(mesh):
    placed = (
        P(("parts", "fsdp"), None),
        P(("parts", "fsdp"), None),
        P(("parts", "fsdp"), "clients"),
        P("fsdp", None),
        P(),
        P(("parts", "fsdp"), None),
        P(("parts", "clients"), "fsdp", None),
    )
    return jax.shard_map(
        per_device,
        mesh=mesh,
        in_specs=placed,
        out_specs=(
            P(("parts", "fsdp"), None),
            P(("parts", "fsdp"), None),
            P(("parts", "clients"), "fsdp", None),
        ),
        check_vma=False,
    )
```

```python
import jax
import jax.numpy as jnp
from jax import lax
from jax.sharding import PartitionSpec as P

HEAD = 128

norm_eps = 1e-06
local_rate = 0.05
CHUNKS = 4


def norm_backward(keys, cotangent, gain):
    count, width = keys.shape
    heads = keys.reshape(count, width // HEAD, HEAD)
    inverse = lax.rsqrt(jnp.mean(heads * heads, axis=-1, keepdims=True) + norm_eps)
    scaled = cotangent.astype(jnp.float32).reshape(heads.shape) * gain
    along = jnp.sum(scaled * heads, axis=-1, keepdims=True)
    result = scaled * inverse - heads * along * inverse * inverse * inverse / HEAD
    return result.reshape(count, width).astype(jnp.bfloat16)


def gather_weight(weight):
    weight_b = weight.astype(jnp.bfloat16)
    rows = weight.shape[0] // lax.axis_size("clients")
    own = lax.dynamic_slice_in_dim(weight_b, lax.axis_index("clients") * rows, rows, 0)
    return lax.all_gather(own, ("fsdp", "clients"), axis=0, tiled=True)


def scatter_sum(partial, before):
    n = lax.axis_size("fsdp")
    lines = n // 2
    me = lax.axis_index("fsdp")
    line, side = me // 2, lax.rem(me, 2)
    rows = partial.shape[0] // n
    blocks = partial.reshape(lines, 2, rows, partial.shape[1])
    away = lax.dynamic_index_in_dim(blocks, 1 - side, 1, keepdims=False)
    home = lax.dynamic_index_in_dim(blocks, side, 1, keepdims=False)
    away = away.astype(jnp.bfloat16)
    ready = lax.optimization_barrier((away, *before))[0] if before else away
    came = lax.ppermute(ready, "fsdp", [(i, i ^ 1) for i in range(n)])
    both = home + came.astype(jnp.float32)
    narrow = both.astype(jnp.bfloat16)
    own = lax.dynamic_index_in_dim(both, line, 0, keepdims=False)
    if lines <= 4:
        total, moved = own, []
        for step in range(1, lines):
            block = lax.dynamic_index_in_dim(
                narrow, lax.rem(line + step, lines), 0, keepdims=False
            )
            pairs = [(i, (i + 2 * step) % n) for i in range(n)]
            got = lax.ppermute(block, "fsdp", pairs)
            moved.append(got)
            total = total + got.astype(jnp.float32)
        return total, narrow, away, moved
    groups = [[2 * z + x for z in range(lines)] for x in range(2)]
    got = lax.all_to_all(
        narrow, "fsdp", 0, 0, axis_index_groups=groups
    ).astype(jnp.float32)
    others = jnp.arange(lines)[:, None, None] != line
    return own + jnp.sum(jnp.where(others, got, 0.0), axis=0), narrow, away, []


def per_device(pool_x, pool_cot, assignment, weight, gain, global_variate, client_variate):
    members = lax.axis_size("clients")
    weight_b = gather_weight(weight)
    picked = assignment[0]
    x_rows = pool_x.at[picked].get(mode="promise_in_bounds")
    cot_rows = pool_cot.at[picked].get(mode="promise_in_bounds")
    width = weight.shape[1] // CHUNKS
    own_variate = client_variate[0]
    results, came, moved = [], [], []
    for chunk in range(CHUNKS):
        cut = slice(chunk * width, (chunk + 1) * width)
        if chunk:
            weight_b = lax.optimization_barrier((weight_b, sent))[0]
        keys = jnp.dot(x_rows, weight_b[:, cut], preferred_element_type=jnp.float32)
        dkeys = norm_backward(keys, cot_rows[:, cut], gain)
        partial = lax.dot_general(
            x_rows, dkeys, (((0,), (0,)), ((), ())), preferred_element_type=jnp.float32
        )
        before = [came[chunk - 1]] if chunk >= 1 else []
        if chunk >= 2:
            before += moved[chunk - 2]
        grads, arrived, sent, along = scatter_sum(partial, before)
        came.append(arrived)
        moved.append(along)
        change = grads - own_variate[:, cut]
        total_change = change
        for step in range(1, members):
            pairs = [(i, (i + step) % members) for i in range(members)]
            total_change = total_change + lax.ppermute(change, "clients", pairs)
        common = global_variate[:, cut]
        total_delta = -local_rate * (total_change + members * common)
        new_weight = weight[:, cut] + total_delta / members
        new_global = common + total_change / members
        results.append((new_weight, new_global, grads))
    new_weight, new_global, grads = (
        jnp.concatenate(list(pieces), axis=1) for pieces in zip(*results)
    )
    return (new_weight, new_global, grads[None])


def solution(mesh):
    placed = (
        P(("parts", "fsdp"), None),
        P(("parts", "fsdp"), None),
        P(("parts", "fsdp"), "clients"),
        P("fsdp", None),
        P(),
        P(("parts", "fsdp"), None),
        P(("parts", "clients"), "fsdp", None),
    )
    return jax.shard_map(
        per_device,
        mesh=mesh,
        in_specs=placed,
        out_specs=(
            P(("parts", "fsdp"), None),
            P(("parts", "fsdp"), None),
            P(("parts", "clients"), "fsdp", None),
        ),
        check_vma=False,
    )
```

```python
import jax
import jax.numpy as jnp
from jax import lax
from jax.sharding import PartitionSpec as P

HEAD = 128

norm_eps = 1e-06
local_rate = 0.05
CHUNKS = 4


def norm_backward(keys, cotangent, gain):
    count, width = keys.shape
    heads = keys.reshape(count, width // HEAD, HEAD)
    inverse = lax.rsqrt(jnp.mean(heads * heads, axis=-1, keepdims=True) + norm_eps)
    scaled = cotangent.astype(jnp.float32).reshape(heads.shape) * gain
    along = jnp.sum(scaled * heads, axis=-1, keepdims=True)
    result = scaled * inverse - heads * along * inverse * inverse * inverse / HEAD
    return result.reshape(count, width).astype(jnp.bfloat16)


def in_order(pieces, me):
    count = len(pieces)
    stacked = jnp.stack(pieces[::-1] + pieces[:0:-1])
    return lax.dynamic_slice_in_dim(stacked, count - 1 - me, count, 0)


def gather_weight(weight, x_rows, cot_rows):
    weight_b = weight.astype(jnp.bfloat16)
    members = lax.axis_size("clients")
    core = lax.axis_index("clients")
    rows = weight.shape[0] // members
    own = lax.dynamic_slice_in_dim(weight_b, core * rows, rows, 0)
    n = lax.axis_size("fsdp")
    lines = n // 2
    if lines > 4:
        whole = lax.all_gather(own, ("fsdp", "clients"), axis=0, tiled=True)
        return jnp.split(whole, 2, axis=1)
    me = lax.axis_index("fsdp")
    line, side = me // 2, lax.rem(me, 2)
    halves = []
    width = weight.shape[1] // 2
    for half in range(2):
        piece = own[:, half * width : (half + 1) * width]
        if half:
            piece = lax.optimization_barrier((piece, cot_rows, *pieces[1:]))[0]
        pieces = [piece]
        for step in range(1, lines):
            pairs = [(i, (i + 2 * step) % n) for i in range(n)]
            pieces.append(lax.ppermute(piece, "fsdp", pairs))
        column = in_order(pieces, line)
        if half:
            column = lax.optimization_barrier((column, x_rows))[0]
        other = lax.ppermute(column, "fsdp", [(i, i ^ 1) for i in range(n)])
        first = jnp.where(side == 0, column, other)
        second = jnp.where(side == 0, other, column)
        plane = jnp.stack([first, second], axis=1)
        cores = [plane]
        for step in range(1, members):
            pairs = [(i, (i + step) % members) for i in range(members)]
            cores.append(lax.ppermute(plane, "clients", pairs))
        ordered = in_order(cores, core)
        halves.append(jnp.moveaxis(ordered, 0, 2).reshape(n * members * rows, width))
    return halves


def scatter_sum(partial, before):
    n = lax.axis_size("fsdp")
    lines = n // 2
    me = lax.axis_index("fsdp")
    line, side = me // 2, lax.rem(me, 2)
    rows = partial.shape[0] // n
    blocks = partial.reshape(lines, 2, rows, partial.shape[1])
    away = lax.dynamic_index_in_dim(blocks, 1 - side, 1, keepdims=False)
    home = lax.dynamic_index_in_dim(blocks, side, 1, keepdims=False)
    away = away.astype(jnp.bfloat16)
    ready = lax.optimization_barrier((away, *before))[0] if before else away
    came = lax.ppermute(ready, "fsdp", [(i, i ^ 1) for i in range(n)])
    both = home + came.astype(jnp.float32)
    narrow = both.astype(jnp.bfloat16)
    own = lax.dynamic_index_in_dim(both, line, 0, keepdims=False)
    if lines <= 4:
        total, moved = own, []
        for step in range(1, lines):
            block = lax.dynamic_index_in_dim(
                narrow, lax.rem(line + step, lines), 0, keepdims=False
            )
            pairs = [(i, (i + 2 * step) % n) for i in range(n)]
            got = lax.ppermute(block, "fsdp", pairs)
            moved.append(got)
            total = total + got.astype(jnp.float32)
        return total, narrow, away, moved
    groups = [[2 * z + x for z in range(lines)] for x in range(2)]
    got = lax.all_to_all(
        narrow, "fsdp", 0, 0, axis_index_groups=groups
    ).astype(jnp.float32)
    others = jnp.arange(lines)[:, None, None] != line
    return own + jnp.sum(jnp.where(others, got, 0.0), axis=0), narrow, away, []


def per_device(pool_x, pool_cot, assignment, weight, gain, global_variate, client_variate):
    members = lax.axis_size("clients")
    picked = assignment[0]
    x_rows = pool_x.at[picked].get(mode="promise_in_bounds")
    cot_rows = pool_cot.at[picked].get(mode="promise_in_bounds")
    weight_b = gather_weight(weight, x_rows, cot_rows)
    width = weight.shape[1] // CHUNKS
    own_variate = client_variate[0]
    results, came, moved = [], [], []
    for chunk in range(CHUNKS):
        cut = slice(chunk * width, (chunk + 1) * width)
        half, place = divmod(chunk, CHUNKS // 2)
        if chunk:
            weight_b[half] = lax.optimization_barrier((weight_b[half], sent))[0]
        weight_c = weight_b[half][:, place * width : (place + 1) * width]
        keys = jnp.dot(x_rows, weight_c, preferred_element_type=jnp.float32)
        dkeys = norm_backward(keys, cot_rows[:, cut], gain)
        partial = lax.dot_general(
            x_rows, dkeys, (((0,), (0,)), ((), ())), preferred_element_type=jnp.float32
        )
        before = [came[chunk - 1]] if chunk >= 1 else []
        if chunk >= 2:
            before += moved[chunk - 2]
        grads, arrived, sent, along = scatter_sum(partial, before)
        came.append(arrived)
        moved.append(along)
        change = grads - own_variate[:, cut]
        total_change = change
        for step in range(1, members):
            pairs = [(i, (i + step) % members) for i in range(members)]
            total_change = total_change + lax.ppermute(change, "clients", pairs)
        common = global_variate[:, cut]
        total_delta = -local_rate * (total_change + members * common)
        new_weight = weight[:, cut] + total_delta / members
        new_global = common + total_change / members
        results.append((new_weight, new_global, grads))
    new_weight, new_global, grads = (
        jnp.concatenate(list(pieces), axis=1) for pieces in zip(*results)
    )
    return (new_weight, new_global, grads[None])


def solution(mesh):
    placed = (
        P(("parts", "fsdp"), None),
        P(("parts", "fsdp"), None),
        P(("parts", "fsdp"), "clients"),
        P("fsdp", None),
        P(),
        P(("parts", "fsdp"), None),
        P(("parts", "clients"), "fsdp", None),
    )
    return jax.shard_map(
        per_device,
        mesh=mesh,
        in_specs=placed,
        out_specs=(
            P(("parts", "fsdp"), None),
            P(("parts", "fsdp"), None),
            P(("parts", "clients"), "fsdp", None),
        ),
        check_vma=False,
    )
```

```python
import jax
import jax.numpy as jnp
from jax import lax
from jax.sharding import PartitionSpec as P

HEAD = 128

norm_eps = 1e-06
local_rate = 0.05
CHUNKS = 4


def norm_backward(keys, cotangent, gain):
    count, width = keys.shape
    heads = keys.reshape(count, width // HEAD, HEAD)
    inverse = lax.rsqrt(jnp.mean(heads * heads, axis=-1, keepdims=True) + norm_eps)
    scaled = cotangent.astype(jnp.float32).reshape(heads.shape) * gain
    along = jnp.sum(scaled * heads, axis=-1, keepdims=True)
    result = scaled * inverse - heads * along * inverse * inverse * inverse / HEAD
    return result.reshape(count, width).astype(jnp.bfloat16)


def in_order(pieces, me):
    count = len(pieces)
    stacked = jnp.stack(pieces[::-1] + pieces[:0:-1])
    return lax.dynamic_slice_in_dim(stacked, count - 1 - me, count, 0)


def gather_weight(weight, x_rows):
    weight_b = weight.astype(jnp.bfloat16)
    members = lax.axis_size("clients")
    core = lax.axis_index("clients")
    rows = weight.shape[0] // members
    own = lax.dynamic_slice_in_dim(weight_b, core * rows, rows, 0)
    n = lax.axis_size("fsdp")
    lines = n // 2
    if lines > 4:
        whole = lax.all_gather(own, ("fsdp", "clients"), axis=0, tiled=True)
        return jnp.split(whole, 2, axis=1)
    me = lax.axis_index("fsdp")
    line, side = me // 2, lax.rem(me, 2)
    halves = []
    width = weight.shape[1] // 2
    for half in range(2):
        piece = own[:, half * width : (half + 1) * width]
        pieces = [piece]
        for step in range(1, lines):
            pairs = [(i, (i + 2 * step) % n) for i in range(n)]
            pieces.append(lax.ppermute(piece, "fsdp", pairs))
        column = in_order(pieces, line)
        if half:
            column = lax.optimization_barrier((column, x_rows, other))[0]
        other = lax.ppermute(column, "fsdp", [(i, i ^ 1) for i in range(n)])
        first = jnp.where(side == 0, column, other)
        second = jnp.where(side == 0, other, column)
        plane = jnp.stack([first, second], axis=1)
        cores = [plane]
        for step in range(1, members):
            pairs = [(i, (i + step) % members) for i in range(members)]
            cores.append(lax.ppermute(plane, "clients", pairs))
        ordered = in_order(cores, core)
        halves.append(jnp.moveaxis(ordered, 0, 2).reshape(n * members * rows, width))
    return halves


def scatter_sum(partial, before):
    n = lax.axis_size("fsdp")
    lines = n // 2
    me = lax.axis_index("fsdp")
    line, side = me // 2, lax.rem(me, 2)
    rows = partial.shape[0] // n
    blocks = partial.reshape(lines, 2, rows, partial.shape[1])
    away = lax.dynamic_index_in_dim(blocks, 1 - side, 1, keepdims=False)
    home = lax.dynamic_index_in_dim(blocks, side, 1, keepdims=False)
    away = away.astype(jnp.bfloat16)
    ready = lax.optimization_barrier((away, *before))[0] if before else away
    came = lax.ppermute(ready, "fsdp", [(i, i ^ 1) for i in range(n)])
    both = home + came.astype(jnp.float32)
    narrow = both.astype(jnp.bfloat16)
    own = lax.dynamic_index_in_dim(both, line, 0, keepdims=False)
    if lines <= 4:
        total, moved = own, []
        for step in range(1, lines):
            block = lax.dynamic_index_in_dim(
                narrow, lax.rem(line + step, lines), 0, keepdims=False
            )
            pairs = [(i, (i + 2 * step) % n) for i in range(n)]
            got = lax.ppermute(block, "fsdp", pairs)
            moved.append(got)
            total = total + got.astype(jnp.float32)
        return total, narrow, away, moved
    groups = [[2 * z + x for z in range(lines)] for x in range(2)]
    got = lax.all_to_all(
        narrow, "fsdp", 0, 0, axis_index_groups=groups
    ).astype(jnp.float32)
    others = jnp.arange(lines)[:, None, None] != line
    return own + jnp.sum(jnp.where(others, got, 0.0), axis=0), narrow, away, []


def per_device(pool_x, pool_cot, assignment, weight, gain, global_variate, client_variate):
    members = lax.axis_size("clients")
    picked = assignment[0]
    x_rows = pool_x.at[picked].get(mode="promise_in_bounds")
    cot_rows = pool_cot.at[picked].get(mode="promise_in_bounds")
    weight_b = gather_weight(weight, x_rows)
    width = weight.shape[1] // CHUNKS
    own_variate = client_variate[0]
    results, came, moved = [], [], []
    for chunk in range(CHUNKS):
        cut = slice(chunk * width, (chunk + 1) * width)
        half, place = divmod(chunk, CHUNKS // 2)
        if chunk:
            weight_b[half] = lax.optimization_barrier((weight_b[half], sent))[0]
        weight_c = weight_b[half][:, place * width : (place + 1) * width]
        keys = jnp.dot(x_rows, weight_c, preferred_element_type=jnp.float32)
        dkeys = norm_backward(keys, cot_rows[:, cut], gain)
        partial = lax.dot_general(
            x_rows, dkeys, (((0,), (0,)), ((), ())), preferred_element_type=jnp.float32
        )
        before = [came[chunk - 1]] if chunk >= 1 else []
        if chunk >= 2:
            before += moved[chunk - 2]
        grads, arrived, sent, along = scatter_sum(partial, before)
        came.append(arrived)
        moved.append(along)
        change = grads - own_variate[:, cut]
        total_change = change
        for step in range(1, members):
            pairs = [(i, (i + step) % members) for i in range(members)]
            total_change = total_change + lax.ppermute(change, "clients", pairs)
        common = global_variate[:, cut]
        total_delta = -local_rate * (total_change + members * common)
        new_weight = weight[:, cut] + total_delta / members
        new_global = common + total_change / members
        results.append((new_weight, new_global, grads))
    new_weight, new_global, grads = (
        jnp.concatenate(list(pieces), axis=1) for pieces in zip(*results)
    )
    return (new_weight, new_global, grads[None])


def solution(mesh):
    placed = (
        P(("parts", "fsdp"), None),
        P(("parts", "fsdp"), None),
        P(("parts", "fsdp"), "clients"),
        P("fsdp", None),
        P(),
        P(("parts", "fsdp"), None),
        P(("parts", "clients"), "fsdp", None),
    )
    return jax.shard_map(
        per_device,
        mesh=mesh,
        in_specs=placed,
        out_specs=(
            P(("parts", "fsdp"), None),
            P(("parts", "fsdp"), None),
            P(("parts", "clients"), "fsdp", None),
        ),
        check_vma=False,
    )
```
